32 devices in a mesh: crops: 2 (over x), rows: 8 (over z, y), cols: 2 (over core).
Axes of the slice: x: 2, y: 2, z: 4, core: 2. Of those that a mesh axis runs over, the one named last changes fastest.
Arguments:
- pair: bfloat16 [1024, 512, 128], P(('crops', 'rows'), 'cols'), parts along dimension 0, may hold values from -6 to 6
- token_mask: int32 [1024], P('crops'), parts along dimension 0, may hold values 0 or 1
- in_gain: float32 [128], replicated, may hold values from 0.25 to 1.75
- left_proj: bfloat16 [128, 128], replicated, may hold values from -0.5 to 0.5
- left_gate: bfloat16 [128, 128], replicated, may hold values from -0.5 to 0.5
- right_proj: bfloat16 [128, 128], replicated, may hold values from -0.5 to 0.5
- right_gate: bfloat16 [128, 128], replicated, may hold values from -0.5 to 0.5
- out_gate: bfloat16 [128, 128], replicated, may hold values from -0.5 to 0.5
- out_gain: float32 [128], replicated, may hold values from 0.25 to 1.75
- out_proj: bfloat16 [128, 128], replicated, may hold values from -0.5 to 0.5
Outputs:
- pair_out: bfloat16 [1024, 512, 128], P(('crops', 'rows'), 'cols'), parts along dimension 0
The draws below stay inside these ranges and needn't reach their ends.
There are 2 independent parts, one for each index of `crops`. The reference program is written for one: setup_inputs(seed, part) draws one part's arguments, and reference() takes and returns one part's arrays. A program takes and returns all parts, laid end to end along the dimension named above; an argument that names none is the same for every part. Nothing has to cross between parts.
Inputs may be any that keep to these rules, and one draw needn't show every extreme that they name: `token_mask`: 1 marks a real token, 0 a padding position.
All inputs are finite; a program needn't handle non-finite values.
Results may differ from the reference program's by a relative error of at most 0.0049.
Values may be sent and summed in bfloat16 or wider, within the bound.
A program may use at most 192 MiB of HBM per device.

```python
import jax
import jax.numpy as jnp
from jax import lax

PAIR_C = 128
HID = 128
CROP = 512


def plant(values, own_key, low, top_value):
    longest = values.shape.index(max(values.shape))
    spots = []
    for shift in (0, 1):
        where = [jax.random.randint(jax.random.fold_in(own_key, axis), (), 0, length) for axis, length in enumerate(values.shape)]
        where[longest] = (where[longest] + shift) % values.shape[longest]
        spots.append(tuple(where))
    return values.at[spots[0]].set(low).at[spots[1]].set(top_value)


def block_levels(key, extent, pieces, smallest, top_value):
    def one(position, shards_of):
        steps = jax.random.uniform(jax.random.fold_in(jax.random.fold_in(key, 6), position), (shards_of,), jnp.float32, smallest / len(pieces), top_value / len(pieces))
        return jnp.repeat(jnp.exp(steps), extent[position] // shards_of).reshape((-1,) + (1,) * (len(extent) - position - 1))

    loudness = one(*pieces[0])
    for cut in pieces[1:]:
        loudness = loudness * one(*cut)
    return loudness


def normal_values(rng, dims, scale, bound, shards=(), kind=jnp.bfloat16):
    values = jax.random.normal(rng, dims, jnp.float32) * scale
    if len(shards) > 0:
        values = block_levels(rng, dims, shards, -0.22, 0.18) * values
    return jnp.clip(values, min=-bound, max=bound).astype(kind)


def setup_inputs(seed: int = 0, part: int = 0) -> dict:
    key_of = jax.random.split(jax.random.key(seed), 11)
    own_keys = jax.random.split(jax.random.fold_in(key_of[10], part), 11)
    return {
        "pair": normal_values(own_keys[0], (CROP, CROP, PAIR_C), 1.0, 6.0, ((0, 8), (1, 2))),
        "token_mask": plant((jax.random.randint(own_keys[1], (CROP,), 0, 8) < 7).astype(jnp.int32), jax.random.fold_in(own_keys[1], 1), 0, 1),
        "in_gain": jnp.clip(1.0 + 0.15 * jax.random.normal(key_of[2], (PAIR_C,), jnp.float32), 0.25, 1.75),
        "left_proj": normal_values(key_of[3], (PAIR_C, HID), PAIR_C ** -0.5, 0.5),
        "left_gate": normal_values(key_of[4], (PAIR_C, HID), PAIR_C ** -0.5, 0.5),
        "right_proj": normal_values(key_of[5], (PAIR_C, HID), PAIR_C ** -0.5, 0.5),
        "right_gate": normal_values(key_of[6], (PAIR_C, HID), PAIR_C ** -0.5, 0.5),
        "out_gate": normal_values(key_of[7], (PAIR_C, PAIR_C), PAIR_C ** -0.5, 0.5),
        "out_gain": jnp.clip(1.0 + 0.15 * jax.random.normal(key_of[8], (HID,), jnp.float32), 0.25, 1.75),
        "out_proj": normal_values(key_of[9], (HID, PAIR_C), HID ** -0.5, 0.5),
    }


def layer_norm(values, gains):
    average = lax.optimization_barrier(jnp.mean(values, axis=-1, keepdims=True))
    centred = values - average
    spread = lax.optimization_barrier(jnp.mean(centred * centred, axis=-1, keepdims=True))
    return centred * lax.rsqrt(spread + 1e-05) * gains

def reference(pair, token_mask, in_gain, left_proj, left_gate, right_proj, right_gate, out_gate, out_gain, out_proj):
    crop_len = pair.shape[0]
    channels = pair.shape[2]
    widened = pair.astype(jnp.float32)
    normed = layer_norm(widened, in_gain.astype(jnp.float32)).astype(jnp.bfloat16)
    flattened = normed.reshape(crop_len * crop_len, channels)
    mask_values = token_mask.astype(jnp.float32)
    pair_mask = (mask_values[:, None] * mask_values[None, :])[:, :, None]

    def project(weight):
        return jnp.dot(flattened, weight, preferred_element_type=jnp.float32).reshape(crop_len, crop_len, -1)
    left_side = (jax.nn.sigmoid(project(left_gate)) * project(left_proj) * pair_mask).astype(jnp.bfloat16)
    right_side = (jax.nn.sigmoid(project(right_gate)) * project(right_proj) * pair_mask).astype(jnp.bfloat16)
    combined = jnp.einsum('ikh,jkh->ijh', left_side.astype(jnp.float32), right_side.astype(jnp.float32), precision=lax.Precision.HIGHEST)
    combined_norm = layer_norm(combined, out_gain.astype(jnp.float32)).astype(jnp.bfloat16)
    gate_values = jax.nn.sigmoid(project(out_gate))
    update = jnp.dot(combined_norm.reshape(crop_len * crop_len, -1), out_proj, preferred_element_type=jnp.float32).reshape(crop_len, crop_len, channels)
    updated = (widened + gate_values * update).astype(jnp.bfloat16)
    return jnp.transpose(updated, (1, 0, 2))
```

```python
import jax
import jax.numpy as jnp
from jax import lax
from jax.sharding import PartitionSpec as P

CHUNKS = 2


def norm_last(values, gains):
    average = jnp.mean(values, axis=-1, keepdims=True)
    centred = values - average
    spread = jnp.mean(centred * centred, axis=-1, keepdims=True)
    return centred * lax.rsqrt(spread + 1e-05) * gains


def norm_first(values, gains):
    average = jnp.mean(values, axis=0, keepdims=True)
    centred = values - average
    spread = jnp.mean(centred * centred, axis=0, keepdims=True)
    return centred * lax.rsqrt(spread + 1e-05) * gains[:, None, None]


def body(
    pair,
    token_mask,
    in_gain,
    left_proj,
    left_gate,
    right_proj,
    right_gate,
    out_gate,
    out_gain,
    out_proj,
):
    n_rows = lax.axis_size("rows")
    n_cols = lax.axis_size("cols")
    assert n_rows % 4 == 0 and n_cols == 2
    n_pairs = n_rows // 2
    half_pairs = n_pairs // 2
    rows_tile, cols_tile, channels = pair.shape
    row_at = lax.axis_index("rows")
    col_at = lax.axis_index("cols")
    pair_at, side_at = row_at // 2, row_at % 2

    mask_values = token_mask.astype(jnp.float32)
    mask_cols = lax.dynamic_slice_in_dim(mask_values, col_at * cols_tile, cols_tile)

    def along(block, step):
        return lax.ppermute(
            block, "rows", [(r, (r + 2 * step) % n_rows) for r in range(n_rows)]
        )

    def across(block):
        return lax.ppermute(block, "rows", [(r, r ^ 1) for r in range(n_rows)])

    def sibling(block):
        return lax.ppermute(block, "cols", [(0, 1), (1, 0)])

    def after(value, *others):
        return lax.optimization_barrier((value, *others))[0]

    order = [d + h * half_pairs for d in range(half_pairs) for h in (0, 1)]
    chunk_rows = rows_tile // CHUNKS
    own = [pair[n * chunk_rows : (n + 1) * chunk_rows] for n in range(CHUNKS)]
    mine, other = {}, {}
    z_queue, y_queue = [], []
    for d in order:
        for n in range(CHUNKS):
            if d == 0:
                mine[d, n] = own[n]
            else:
                source = own[n] if len(z_queue) < 2 else after(own[n], z_queue[-2])
                mine[d, n] = along(source, d)
                z_queue.append(mine[d, n])
            source = mine[d, n] if len(y_queue) < 2 else after(mine[d, n], y_queue[-2])
            other[d, n] = across(source)
            y_queue.append(other[d, n])

    def gated(normed, w_proj, w_gate, pair_mask):
        projected = jnp.einsum("xkd,dh->hxk", normed, w_proj, preferred_element_type=jnp.float32)
        gate_logits = jnp.einsum("xkd,dh->hxk", normed, w_gate, preferred_element_type=jnp.float32)
        return (jax.nn.sigmoid(gate_logits) * projected * pair_mask[None]).astype(jnp.bfloat16)

    def normalise(values):
        return norm_last(values.astype(jnp.float32), in_gain).astype(jnp.bfloat16)

    mask_rows = lax.dynamic_slice_in_dim(mask_values, row_at * rows_tile, rows_tile)
    right_side = gated(
        normalise(pair), right_proj, right_gate, mask_rows[:, None] * mask_cols[None, :]
    )
    width = 2 * rows_tile

    def block_of(d):
        held = jnp.concatenate([mine[d, n] for n in range(CHUNKS)], axis=0)
        swapped = jnp.concatenate([other[d, n] for n in range(CHUNKS)], axis=0)
        first = jnp.where(side_at == 0, held, swapped)
        second = jnp.where(side_at == 0, swapped, held)
        return jnp.concatenate([first, second], axis=0)

    def source_pair(d):
        return lax.rem(pair_at - d + n_pairs, n_pairs)

    def product(block, d):
        rows_mask = lax.dynamic_slice_in_dim(mask_values, source_pair(d) * width, width)
        left_side = gated(
            normalise(block), left_proj, left_gate, rows_mask[:, None] * mask_cols[None, :]
        )
        return jnp.einsum("hxk,hyk->hyx", left_side, right_side, preferred_element_type=jnp.float32)

    column_at = lax.rem(row_at * rows_tile, cols_tile)
    column_core = (row_at * rows_tile) // cols_tile

    out = jnp.zeros((rows_tile, cols_tile, channels), jnp.bfloat16)
    for d in range(half_pairs):
        near, far = block_of(d), block_of(d + half_pairs)
        keep_near = source_pair(d) // half_pairs == col_at
        near_pair = lax.dynamic_slice_in_dim(near, column_at, rows_tile, 1)
        far_pair = lax.dynamic_slice_in_dim(far, column_at, rows_tile, 1)
        kept_pair = jnp.where(keep_near, near_pair, far_pair)
        got_pair = sibling(jnp.where(keep_near, far_pair, near_pair))
        turned = jnp.where(column_core == col_at, kept_pair, got_pair)
        gate_values = jax.nn.sigmoid(
            jnp.einsum(
                "ijd,dc->jic", normalise(turned), out_gate, preferred_element_type=jnp.float32
            )
        )
        near_sum, far_sum = product(near, d), product(far, d + half_pairs)
        got_sum = sibling(jnp.where(keep_near, far_sum, near_sum).astype(jnp.bfloat16))
        combined = jnp.where(keep_near, near_sum, far_sum) + got_sum.astype(jnp.float32)
        combined_norm = norm_first(combined, out_gain).astype(jnp.bfloat16)
        update = jnp.einsum(
            "hji,hd->jid", combined_norm, out_proj, preferred_element_type=jnp.float32
        )
        swapped = jnp.transpose(turned, (1, 0, 2)).astype(jnp.float32)
        result = (swapped + gate_values * update).astype(jnp.bfloat16)
        place = lax.rem(pair_at - d + n_pairs, half_pairs)
        out = lax.dynamic_update_slice(out, result, (0, place * width, 0))
    return out


def solution(mesh):
    return jax.shard_map(
        body,
        mesh=mesh,
        in_specs=(
            P(("crops", "rows"), "cols", None),
            P("crops"),
            P(),
            P(),
            P(),
            P(),
            P(),
            P(),
            P(),
            P(),
        ),
        out_specs=P(("crops", "rows"), "cols", None),
        check_vma=False,
    )
```

```python
import functools

import jax
import jax.numpy as jnp
from jax import lax
from jax.experimental import pallas as pl
from jax.experimental.pallas import tpu as pltpu
from jax.sharding import PartitionSpec as P

CHUNKS = 2
STEP = 16


def left_kernel(parts, steps, place_ref, *refs):
    blocks = refs[:parts]
    mask_ref, gain_ref, weight_ref, right_ref, out_ref, active, slab, left = refs[parts:]
    at = pl.program_id(0)
    for part in range(parts):

        @pl.when(at // steps == part)
        def _():
            active[...] = blocks[part][...]

    hidden = weight_ref.shape[0] // 2
    gain = gain_ref[...]
    base = pl.multiple_of(lax.rem(at * STEP + place_ref[0], left.shape[1]), STEP)

    def row(x, carry):
        normed = norm_last(active[x].astype(jnp.float32), gain).astype(jnp.bfloat16)
        both = lax.dot_general(
            weight_ref[...], normed, (((1,), (1,)), ((), ())), preferred_element_type=jnp.float32
        )
        gate = 0.5 * jnp.tanh(0.5 * both[hidden:]) + 0.5
        slab[x] = gate * (both[:hidden] * mask_ref[pl.ds(base + x, 1), :])
        return carry

    lax.fori_loop(0, STEP, row, None, unroll=4)
    for c in range(0, hidden, 16):
        left[c : c + 16, pl.ds(base, STEP), :] = jnp.swapaxes(slab[:, c : c + 16, :], 0, 1).astype(
            jnp.bfloat16
        )

    @pl.when(at == parts * steps - 1)
    def _():
        def head(h, carry):
            out_ref[h] = lax.dot_general(
                right_ref[h], left[h], (((1,), (1,)), ((), ())), preferred_element_type=jnp.float32
            )
            return carry

        lax.fori_loop(0, hidden, head, None, unroll=4)


def left_product(blocks, place, mask, gain, weight, right):
    parts = len(blocks)
    rows, depth, channels = blocks[0].shape
    steps = rows // STEP
    hidden, wide, _ = right.shape
    width = parts * rows

    def part_spec(part):
        return pl.BlockSpec(
            (STEP, depth, channels), lambda g, p: (jnp.clip(g - part * steps, 0, steps - 1), 0, 0)
        )

    def whole(a):
        return pl.BlockSpec(a.shape, lambda g, p: (0,) * a.ndim)

    return pl.pallas_call(
        functools.partial(left_kernel, parts, steps),
        grid_spec=pltpu.PrefetchScalarGridSpec(
            num_scalar_prefetch=1,
            grid=(parts * steps,),
            in_specs=[part_spec(i) for i in range(parts)]
            + [whole(mask), whole(gain), whole(weight), whole(right)],
            out_specs=pl.BlockSpec((hidden, wide, width), lambda g, p: (0, 0, 0)),
            scratch_shapes=[
                pltpu.VMEM((STEP, depth, channels), jnp.bfloat16),
                pltpu.VMEM((STEP, hidden, depth), jnp.float32),
                pltpu.VMEM((hidden, width, depth), jnp.bfloat16),
            ],
        ),
        out_shape=jax.ShapeDtypeStruct((hidden, wide, width), jnp.float32),
        compiler_params=pltpu.CompilerParams(
            vmem_limit_bytes=50 * 2**20, dimension_semantics=("arbitrary",)
        ),
        cost_estimate=pl.CostEstimate(
            flops=2 * width * depth * (channels * 2 * hidden + hidden * wide),
            bytes_accessed=20 * 2**20,
            transcendentals=width * depth * hidden,
        ),
    )(place, *blocks, mask, gain, weight, right)


def norm_last(values, gains):
    average = jnp.mean(values, axis=-1, keepdims=True)
    centred = values - average
    spread = jnp.mean(centred * centred, axis=-1, keepdims=True)
    return centred * lax.rsqrt(spread + 1e-05) * gains


def norm_first(values, gains):
    average = jnp.mean(values, axis=0, keepdims=True)
    centred = values - average
    spread = jnp.mean(centred * centred, axis=0, keepdims=True)
    return centred * lax.rsqrt(spread + 1e-05) * gains[:, None, None]


def body(
    pair,
    token_mask,
    in_gain,
    left_proj,
    left_gate,
    right_proj,
    right_gate,
    out_gate,
    out_gain,
    out_proj,
):
    n_rows = lax.axis_size("rows")
    n_cols = lax.axis_size("cols")
    assert n_rows % 4 == 0 and n_cols == 2
    n_pairs = n_rows // 2
    half_pairs = n_pairs // 2
    rows_tile, cols_tile, channels = pair.shape
    row_at = lax.axis_index("rows")
    col_at = lax.axis_index("cols")
    pair_at, side_at = row_at // 2, row_at % 2

    mask_values = token_mask.astype(jnp.float32)
    mask_cols = lax.dynamic_slice_in_dim(mask_values, col_at * cols_tile, cols_tile)

    def along(block, step):
        return lax.ppermute(
            block, "rows", [(r, (r + 2 * step) % n_rows) for r in range(n_rows)]
        )

    def across(block):
        return lax.ppermute(block, "rows", [(r, r ^ 1) for r in range(n_rows)])

    def sibling(block):
        return lax.ppermute(block, "cols", [(0, 1), (1, 0)])

    def after(value, *others):
        return lax.optimization_barrier((value, *others))[0]

    order = [d + h * half_pairs for d in range(half_pairs) for h in (0, 1)]
    chunk_rows = rows_tile // CHUNKS
    own = [pair[n * chunk_rows : (n + 1) * chunk_rows] for n in range(CHUNKS)]
    mine, other = {}, {}
    z_queue, y_queue = [], []
    for d in order:
        for n in range(CHUNKS):
            if d == 0:
                mine[d, n] = own[n]
            else:
                source = own[n] if len(z_queue) < 2 else after(own[n], z_queue[-2])
                mine[d, n] = along(source, d)
                z_queue.append(mine[d, n])
            source = mine[d, n] if len(y_queue) < 2 else after(mine[d, n], y_queue[-2])
            other[d, n] = across(source)
            y_queue.append(other[d, n])

    def gated(normed, w_proj, w_gate, pair_mask):
        projected = jnp.einsum("xkd,dh->hxk", normed, w_proj, preferred_element_type=jnp.float32)
        gate_logits = jnp.einsum("xkd,dh->hxk", normed, w_gate, preferred_element_type=jnp.float32)
        return (jax.nn.sigmoid(gate_logits) * projected * pair_mask[None]).astype(jnp.bfloat16)

    def normalise(values):
        return norm_last(values.astype(jnp.float32), in_gain).astype(jnp.bfloat16)

    mask_rows = lax.dynamic_slice_in_dim(mask_values, row_at * rows_tile, rows_tile)
    right_side = gated(
        normalise(pair), right_proj, right_gate, mask_rows[:, None] * mask_cols[None, :]
    )
    width = 2 * rows_tile

    left_weight = jnp.concatenate([left_proj, left_gate], axis=1).T
    place = (side_at * rows_tile).astype(jnp.int32)[None]

    def source_pair(d):
        return lax.rem(pair_at - d + n_pairs, n_pairs)

    def product(d):
        rows_mask = lax.dynamic_slice_in_dim(mask_values, source_pair(d) * width, width)
        blocks = [mine[d, n] for n in range(CHUNKS)] + [other[d, n] for n in range(CHUNKS)]
        return left_product(
            blocks,
            place,
            rows_mask[:, None] * mask_cols[None, :],
            in_gain[None],
            left_weight,
            right_side,
        )

    column_at = lax.rem(row_at * rows_tile, cols_tile)
    column_core = (row_at * rows_tile) // cols_tile

    def columns_of(d):
        def cut(chunks):
            return jnp.concatenate(
                [lax.dynamic_slice_in_dim(c, column_at, rows_tile, 1) for c in chunks], axis=0
            )

        held = cut([mine[d, n] for n in range(CHUNKS)])
        swapped = cut([other[d, n] for n in range(CHUNKS)])
        first = jnp.where(side_at == 0, held, swapped)
        second = jnp.where(side_at == 0, swapped, held)
        return jnp.concatenate([first, second], axis=0)

    out = jnp.zeros((rows_tile, cols_tile, channels), jnp.bfloat16)
    for d in range(half_pairs):
        keep_near = source_pair(d) // half_pairs == col_at
        near_pair, far_pair = columns_of(d), columns_of(d + half_pairs)
        kept_pair = jnp.where(keep_near, near_pair, far_pair)
        got_pair = sibling(jnp.where(keep_near, far_pair, near_pair))
        turned = jnp.where(column_core == col_at, kept_pair, got_pair)
        gate_values = jax.nn.sigmoid(
            jnp.einsum(
                "ijd,dc->jic", normalise(turned), out_gate, preferred_element_type=jnp.float32
            )
        )
        near_sum, far_sum = product(d), product(d + half_pairs)
        got_sum = sibling(jnp.where(keep_near, far_sum, near_sum).astype(jnp.bfloat16))
        combined = jnp.where(keep_near, near_sum, far_sum) + got_sum.astype(jnp.float32)
        combined_norm = norm_first(combined, out_gain).astype(jnp.bfloat16)
        update = jnp.einsum(
            "hji,hd->jid", combined_norm, out_proj, preferred_element_type=jnp.float32
        )
        swapped = jnp.transpose(turned, (1, 0, 2)).astype(jnp.float32)
        result = (swapped + gate_values * update).astype(jnp.bfloat16)
        spot = lax.rem(pair_at - d + n_pairs, half_pairs)
        out = lax.dynamic_update_slice(out, result, (0, spot * width, 0))
    return out


def solution(mesh):
    return jax.shard_map(
        body,
        mesh=mesh,
        in_specs=(
            P(("crops", "rows"), "cols", None),
            P("crops"),
            P(),
            P(),
            P(),
            P(),
            P(),
            P(),
            P(),
            P(),
        ),
        out_specs=P(("crops", "rows"), "cols", None),
        check_vma=False,
    )
```

```python
import functools

import jax
import jax.numpy as jnp
from jax import lax
from jax.experimental import pallas as pl
from jax.experimental.pallas import tpu as pltpu
from jax.sharding import PartitionSpec as P

CHUNKS = 2
STEP = 16


def left_kernel(parts, steps, place_ref, *refs):
    blocks = refs[:parts]
    mask_ref, gain_ref, weight_ref, right_ref, out_ref, active, slab, left = refs[parts:]
    at = pl.program_id(0)
    for part in range(parts):

        @pl.when(at // steps == part)
        def _():
            active[...] = blocks[part][...]

    hidden = weight_ref.shape[0] // 2
    gain = gain_ref[...]
    base = pl.multiple_of(lax.rem(at * STEP + place_ref[0], left.shape[1]), STEP)

    def row(x, carry):
        normed = norm_last(active[x].astype(jnp.float32), gain).astype(jnp.bfloat16)
        both = lax.dot_general(
            weight_ref[...], normed, (((1,), (1,)), ((), ())), preferred_element_type=jnp.float32
        )
        gate = 0.5 * jnp.tanh(0.5 * both[hidden:]) + 0.5
        slab[x] = gate * (both[:hidden] * mask_ref[pl.ds(base + x, 1), :])
        return carry

    lax.fori_loop(0, STEP, row, None, unroll=4)
    for c in range(0, hidden, 16):
        left[c : c + 16, pl.ds(base, STEP), :] = jnp.swapaxes(slab[:, c : c + 16, :], 0, 1).astype(
            jnp.bfloat16
        )

    @pl.when(at == parts * steps - 1)
    def _():
        def head(h, carry):
            out_ref[h] = lax.dot_general(
                right_ref[h], left[h], (((1,), (1,)), ((), ())), preferred_element_type=jnp.float32
            )
            return carry

        lax.fori_loop(0, hidden, head, None, unroll=4)


def left_product(blocks, place, mask, gain, weight, right):
    parts = len(blocks)
    rows, depth, channels = blocks[0].shape
    steps = rows // STEP
    hidden, wide, _ = right.shape
    width = parts * rows

    def part_spec(part):
        return pl.BlockSpec(
            (STEP, depth, channels), lambda g, p: (jnp.clip(g - part * steps, 0, steps - 1), 0, 0)
        )

    def whole(a):
        return pl.BlockSpec(a.shape, lambda g, p: (0,) * a.ndim)

    return pl.pallas_call(
        functools.partial(left_kernel, parts, steps),
        grid_spec=pltpu.PrefetchScalarGridSpec(
            num_scalar_prefetch=1,
            grid=(parts * steps,),
            in_specs=[part_spec(i) for i in range(parts)]
            + [whole(mask), whole(gain), whole(weight), whole(right)],
            out_specs=pl.BlockSpec((hidden, wide, width), lambda g, p: (0, 0, 0)),
            scratch_shapes=[
                pltpu.VMEM((STEP, depth, channels), jnp.bfloat16),
                pltpu.VMEM((STEP, hidden, depth), jnp.float32),
                pltpu.VMEM((hidden, width, depth), jnp.bfloat16),
            ],
        ),
        out_shape=jax.ShapeDtypeStruct((hidden, wide, width), jnp.float32),
        compiler_params=pltpu.CompilerParams(
            vmem_limit_bytes=50 * 2**20, dimension_semantics=("arbitrary",)
        ),
        cost_estimate=pl.CostEstimate(
            flops=32 * width * depth * (channels * 2 * hidden + hidden * wide),
            bytes_accessed=20 * 2**20,
            transcendentals=width * depth * hidden,
        ),
    )(place, *blocks, mask, gain, weight, right)


def norm_last(values, gains):
    average = jnp.mean(values, axis=-1, keepdims=True)
    centred = values - average
    spread = jnp.mean(centred * centred, axis=-1, keepdims=True)
    return centred * lax.rsqrt(spread + 1e-05) * gains


def norm_first(values, gains):
    average = jnp.mean(values, axis=0, keepdims=True)
    centred = values - average
    spread = jnp.mean(centred * centred, axis=0, keepdims=True)
    return centred * lax.rsqrt(spread + 1e-05) * gains[:, None, None]


def body(
    pair,
    token_mask,
    in_gain,
    left_proj,
    left_gate,
    right_proj,
    right_gate,
    out_gate,
    out_gain,
    out_proj,
):
    n_rows = lax.axis_size("rows")
    n_cols = lax.axis_size("cols")
    assert n_rows % 4 == 0 and n_cols == 2
    n_pairs = n_rows // 2
    half_pairs = n_pairs // 2
    rows_tile, cols_tile, channels = pair.shape
    row_at = lax.axis_index("rows")
    col_at = lax.axis_index("cols")
    pair_at, side_at = row_at // 2, row_at % 2

    mask_values = token_mask.astype(jnp.float32)
    mask_cols = lax.dynamic_slice_in_dim(mask_values, col_at * cols_tile, cols_tile)

    def along(block, step):
        return lax.ppermute(
            block, "rows", [(r, (r + 2 * step) % n_rows) for r in range(n_rows)]
        )

    def across(block):
        return lax.ppermute(block, "rows", [(r, r ^ 1) for r in range(n_rows)])

    def sibling(block):
        return lax.ppermute(block, "cols", [(0, 1), (1, 0)])

    chunk_rows = rows_tile // CHUNKS
    own = [pair[n * chunk_rows : (n + 1) * chunk_rows] for n in range(CHUNKS)]
    mine, other = {}, {}
    for d in range(n_pairs):
        for n in range(CHUNKS):
            mine[d, n] = own[n] if d == 0 else along(mine[d - 1, n], 1)
            other[d, n] = across(mine[d, n])

    def gated(normed, w_proj, w_gate, pair_mask):
        projected = jnp.einsum("xkd,dh->hxk", normed, w_proj, preferred_element_type=jnp.float32)
        gate_logits = jnp.einsum("xkd,dh->hxk", normed, w_gate, preferred_element_type=jnp.float32)
        return (jax.nn.sigmoid(gate_logits) * projected * pair_mask[None]).astype(jnp.bfloat16)

    def normalise(values):
        return norm_last(values.astype(jnp.float32), in_gain).astype(jnp.bfloat16)

    mask_rows = lax.dynamic_slice_in_dim(mask_values, row_at * rows_tile, rows_tile)
    right_side = gated(
        normalise(pair), right_proj, right_gate, mask_rows[:, None] * mask_cols[None, :]
    )
    width = 2 * rows_tile

    left_weight = jnp.concatenate([left_proj, left_gate], axis=1).T
    place = (side_at * rows_tile).astype(jnp.int32)[None]

    def source_pair(d):
        return lax.rem(pair_at - d + n_pairs, n_pairs)

    def product(d):
        rows_mask = lax.dynamic_slice_in_dim(mask_values, source_pair(d) * width, width)
        blocks = [mine[d, n] for n in range(CHUNKS)] + [other[d, n] for n in range(CHUNKS)]
        return left_product(
            blocks,
            place,
            rows_mask[:, None] * mask_cols[None, :],
            in_gain[None],
            left_weight,
            right_side,
        )

    column_at = lax.rem(row_at * rows_tile, cols_tile)
    column_core = (row_at * rows_tile) // cols_tile

    def columns_of(d):
        def cut(chunks):
            return jnp.concatenate(
                [lax.dynamic_slice_in_dim(c, column_at, rows_tile, 1) for c in chunks], axis=0
            )

        held = cut([mine[d, n] for n in range(CHUNKS)])
        swapped = cut([other[d, n] for n in range(CHUNKS)])
        first = jnp.where(side_at == 0, held, swapped)
        second = jnp.where(side_at == 0, swapped, held)
        return jnp.concatenate([first, second], axis=0)

    products = [product(d) for d in range(n_pairs)]
    out = jnp.zeros((rows_tile, cols_tile, channels), jnp.bfloat16)
    for d in range(half_pairs):
        keep_near = source_pair(d) // half_pairs == col_at
        near_pair, far_pair = columns_of(d), columns_of(d + half_pairs)
        kept_pair = jnp.where(keep_near, near_pair, far_pair)
        got_pair = sibling(jnp.where(keep_near, far_pair, near_pair))
        turned = jnp.where(column_core == col_at, kept_pair, got_pair)
        gate_values = jax.nn.sigmoid(
            jnp.einsum(
                "ijd,dc->jic", normalise(turned), out_gate, preferred_element_type=jnp.float32
            )
        )
        near_sum, far_sum = products[d], products[d + half_pairs]
        got_sum = sibling(jnp.where(keep_near, far_sum, near_sum).astype(jnp.bfloat16))
        combined = jnp.where(keep_near, near_sum, far_sum) + got_sum.astype(jnp.float32)
        combined_norm = norm_first(combined, out_gain).astype(jnp.bfloat16)
        update = jnp.einsum(
            "hji,hd->jid", combined_norm, out_proj, preferred_element_type=jnp.float32
        )
        swapped = jnp.transpose(turned, (1, 0, 2)).astype(jnp.float32)
        result = (swapped + gate_values * update).astype(jnp.bfloat16)
        spot = lax.rem(pair_at - d + n_pairs, half_pairs)
        out = lax.dynamic_update_slice(out, result, (0, spot * width, 0))
    return out


def solution(mesh):
    return jax.shard_map(
        body,
        mesh=mesh,
        in_specs=(
            P(("crops", "rows"), "cols", None),
            P("crops"),
            P(),
            P(),
            P(),
            P(),
            P(),
            P(),
            P(),
            P(),
        ),
        out_specs=P(("crops", "rows"), "cols", None),
        check_vma=False,
    )
```

```python
import functools

import jax
import jax.numpy as jnp
from jax import lax
from jax.experimental import pallas as pl
from jax.experimental.pallas import tpu as pltpu
from jax.sharding import PartitionSpec as P

CHUNKS = 2
STEP = 16


def left_kernel(parts, steps, place_ref, *refs):
    blocks = refs[:parts]
    mask_ref, gain_ref, weight_ref, right_ref, out_ref, active, slab, left = refs[parts:]
    at = pl.program_id(0)
    for part in range(parts):

        @pl.when(at // steps == part)
        def _():
            active[...] = blocks[part][...]

    hidden = weight_ref.shape[0] // 2
    gain = gain_ref[...]
    base = pl.multiple_of(lax.rem(at * STEP + place_ref[0], left.shape[1]), STEP)

    def row(x, carry):
        normed = norm_last(active[x].astype(jnp.float32), gain).astype(jnp.bfloat16)
        both = lax.dot_general(
            weight_ref[...], normed, (((1,), (1,)), ((), ())), preferred_element_type=jnp.float32
        )
        gate = 0.5 * jnp.tanh(0.5 * both[hidden:]) + 0.5
        slab[x] = gate * (both[:hidden] * mask_ref[pl.ds(base + x, 1), :])
        return carry

    lax.fori_loop(0, STEP, row, None, unroll=4)
    for c in range(0, hidden, 16):
        left[c : c + 16, pl.ds(base, STEP), :] = jnp.swapaxes(slab[:, c : c + 16, :], 0, 1).astype(
            jnp.bfloat16
        )

    @pl.when(at == parts * steps - 1)
    def _():
        def head(h, carry):
            out_ref[h] = lax.dot_general(
                right_ref[h], left[h], (((1,), (1,)), ((), ())), preferred_element_type=jnp.float32
            )
            return carry

        lax.fori_loop(0, hidden, head, None, unroll=4)


def left_product(blocks, place, mask, gain, weight, right):
    parts = len(blocks)
    rows, depth, channels = blocks[0].shape
    steps = rows // STEP
    hidden, wide, _ = right.shape
    width = parts * rows

    def part_spec(part):
        return pl.BlockSpec(
            (STEP, depth, channels), lambda g, p: (jnp.clip(g - part * steps, 0, steps - 1), 0, 0)
        )

    def whole(a):
        return pl.BlockSpec(a.shape, lambda g, p: (0,) * a.ndim)

    return pl.pallas_call(
        functools.partial(left_kernel, parts, steps),
        grid_spec=pltpu.PrefetchScalarGridSpec(
            num_scalar_prefetch=1,
            grid=(parts * steps,),
            in_specs=[part_spec(i) for i in range(parts)]
            + [whole(mask), whole(gain), whole(weight), whole(right)],
            out_specs=pl.BlockSpec((hidden, wide, width), lambda g, p: (0, 0, 0)),
            scratch_shapes=[
                pltpu.VMEM((STEP, depth, channels), jnp.bfloat16),
                pltpu.VMEM((STEP, hidden, depth), jnp.float32),
                pltpu.VMEM((hidden, width, depth), jnp.bfloat16),
            ],
        ),
        out_shape=jax.ShapeDtypeStruct((hidden, wide, width), jnp.float32),
        compiler_params=pltpu.CompilerParams(
            vmem_limit_bytes=50 * 2**20, dimension_semantics=("arbitrary",)
        ),
        cost_estimate=pl.CostEstimate(
            flops=32 * width * depth * (channels * 2 * hidden + hidden * wide),
            bytes_accessed=20 * 2**20,
            transcendentals=width * depth * hidden,
        ),
    )(place, *blocks, mask, gain, weight, right)


def norm_last(values, gains):
    average = jnp.mean(values, axis=-1, keepdims=True)
    centred = values - average
    spread = jnp.mean(centred * centred, axis=-1, keepdims=True)
    return centred * lax.rsqrt(spread + 1e-05) * gains


def norm_first(values, gains):
    average = jnp.mean(values, axis=0, keepdims=True)
    centred = values - average
    spread = jnp.mean(centred * centred, axis=0, keepdims=True)
    return centred * lax.rsqrt(spread + 1e-05) * gains[:, None, None]


def body(
    pair,
    token_mask,
    in_gain,
    left_proj,
    left_gate,
    right_proj,
    right_gate,
    out_gate,
    out_gain,
    out_proj,
):
    n_rows = lax.axis_size("rows")
    n_cols = lax.axis_size("cols")
    assert n_rows % 4 == 0 and n_cols == 2
    n_pairs = n_rows // 2
    half_pairs = n_pairs // 2
    rows_tile, cols_tile, channels = pair.shape
    row_at = lax.axis_index("rows")
    col_at = lax.axis_index("cols")
    pair_at, side_at = row_at // 2, row_at % 2

    mask_values = token_mask.astype(jnp.float32)
    mask_cols = lax.dynamic_slice_in_dim(mask_values, col_at * cols_tile, cols_tile)

    def along(block, step):
        return lax.ppermute(
            block, "rows", [(r, (r + 2 * step) % n_rows) for r in range(n_rows)]
        )

    def across(block):
        return lax.ppermute(block, "rows", [(r, r ^ 1) for r in range(n_rows)])

    def sibling(block):
        return lax.ppermute(block, "cols", [(0, 1), (1, 0)])

    chunk_rows = rows_tile // CHUNKS
    own = [pair[n * chunk_rows : (n + 1) * chunk_rows] for n in range(CHUNKS)]
    mine, other = {}, {}
    for d in range(n_pairs):
        for n in range(CHUNKS):
            mine[d, n] = own[n] if d == 0 else along(mine[d - 1, n], 1)
            other[d, n] = across(mine[d, n])

    def gated(normed, w_proj, w_gate, pair_mask):
        projected = jnp.einsum("xkd,dh->hxk", normed, w_proj, preferred_element_type=jnp.float32)
        gate_logits = jnp.einsum("xkd,dh->hxk", normed, w_gate, preferred_element_type=jnp.float32)
        return (jax.nn.sigmoid(gate_logits) * projected * pair_mask[None]).astype(jnp.bfloat16)

    def normalise(values):
        return norm_last(values.astype(jnp.float32), in_gain).astype(jnp.bfloat16)

    mask_rows = lax.dynamic_slice_in_dim(mask_values, row_at * rows_tile, rows_tile)
    right_side = gated(
        normalise(pair), right_proj, right_gate, mask_rows[:, None] * mask_cols[None, :]
    )
    width = 2 * rows_tile

    left_weight = jnp.concatenate([left_proj, left_gate], axis=1).T
    place = (side_at * rows_tile).astype(jnp.int32)[None]

    def source_pair(d):
        return lax.rem(pair_at - d + n_pairs, n_pairs)

    def halves(d):
        mine_at = source_pair(d) * width + side_at * rows_tile
        other_at = source_pair(d) * width + (1 - side_at) * rows_tile
        return (mine, mine_at), (other, other_at)

    def product_of(d, held, first_row, spot):
        rows_mask = lax.dynamic_slice_in_dim(mask_values, first_row, rows_tile)
        return left_product(
            [held[d, n] for n in range(CHUNKS)],
            spot,
            rows_mask[:, None] * mask_cols[None, :],
            in_gain[None],
            left_weight,
            right_side,
        )

    def product(d):
        rows_mask = lax.dynamic_slice_in_dim(mask_values, source_pair(d) * width, width)
        blocks = [mine[d, n] for n in range(CHUNKS)] + [other[d, n] for n in range(CHUNKS)]
        return left_product(
            blocks,
            place,
            rows_mask[:, None] * mask_cols[None, :],
            in_gain[None],
            left_weight,
            right_side,
        )

    def last_product(d, earlier):
        start = jnp.zeros((1,), jnp.int32)
        later = lax.optimization_barrier((start, earlier))[0]
        (held, held_at), (swapped, swapped_at) = halves(d)
        held_sum = product_of(d, held, held_at, start)
        swapped_sum = product_of(d, swapped, swapped_at, later)
        first = jnp.where(side_at == 0, held_sum, swapped_sum)
        second = jnp.where(side_at == 0, swapped_sum, held_sum)
        return jnp.concatenate([first, second], axis=2)

    column_at = lax.rem(row_at * rows_tile, cols_tile)
    column_core = (row_at * rows_tile) // cols_tile

    def columns_of(d):
        def cut(chunks):
            return jnp.concatenate(
                [lax.dynamic_slice_in_dim(c, column_at, rows_tile, 1) for c in chunks], axis=0
            )

        held = cut([mine[d, n] for n in range(CHUNKS)])
        swapped = cut([other[d, n] for n in range(CHUNKS)])
        first = jnp.where(side_at == 0, held, swapped)
        second = jnp.where(side_at == 0, swapped, held)
        return jnp.concatenate([first, second], axis=0)

    products = [product(d) for d in range(n_pairs - 1)]
    out = jnp.zeros((rows_tile, cols_tile, channels), jnp.bfloat16)
    for d in range(half_pairs):
        keep_near = source_pair(d) // half_pairs == col_at
        near_pair, far_pair = columns_of(d), columns_of(d + half_pairs)
        kept_pair = jnp.where(keep_near, near_pair, far_pair)
        got_pair = sibling(jnp.where(keep_near, far_pair, near_pair))
        turned = jnp.where(column_core == col_at, kept_pair, got_pair)
        gate_values = jax.nn.sigmoid(
            jnp.einsum(
                "ijd,dc->jic", normalise(turned), out_gate, preferred_element_type=jnp.float32
            )
        )
        if d == half_pairs - 1:
            products.append(last_product(n_pairs - 1, out))
        near_sum, far_sum = products[d], products[d + half_pairs]
        got_sum = sibling(jnp.where(keep_near, far_sum, near_sum).astype(jnp.bfloat16))
        combined = jnp.where(keep_near, near_sum, far_sum) + got_sum.astype(jnp.float32)
        combined_norm = norm_first(combined, out_gain).astype(jnp.bfloat16)
        update = jnp.einsum(
            "hji,hd->jid", combined_norm, out_proj, preferred_element_type=jnp.float32
        )
        swapped = jnp.transpose(turned, (1, 0, 2)).astype(jnp.float32)
        result = (swapped + gate_values * update).astype(jnp.bfloat16)
        spot = lax.rem(pair_at - d + n_pairs, half_pairs)
        out = lax.dynamic_update_slice(out, result, (0, spot * width, 0))
    return out


def solution(mesh):
    return jax.shard_map(
        body,
        mesh=mesh,
        in_specs=(
            P(("crops", "rows"), "cols", None),
            P("crops"),
            P(),
            P(),
            P(),
            P(),
            P(),
            P(),
            P(),
            P(),
        ),
        out_specs=P(("crops", "rows"), "cols", None),
        check_vma=False,
    )
```

```python
import functools

import jax
import jax.numpy as jnp
from jax import lax
from jax.experimental import pallas as pl
from jax.experimental.pallas import tpu as pltpu
from jax.sharding import PartitionSpec as P

CHUNKS = 2
STEP = 16


def left_kernel(parts, steps, place_ref, *refs):
    blocks = refs[:parts]
    mask_ref, gain_ref, weight_ref, right_ref, out_ref, active, slab, left = refs[parts:]
    at = pl.program_id(0)
    for part in range(parts):

        @pl.when(at // steps == part)
        def _():
            active[...] = blocks[part][...]

    hidden = weight_ref.shape[0] // 2
    gain = gain_ref[...]
    base = pl.multiple_of(lax.rem(at * STEP + place_ref[0], left.shape[1]), STEP)

    def row(x, carry):
        normed = norm_last(active[x].astype(jnp.float32), gain).astype(jnp.bfloat16)
        both = lax.dot_general(
            weight_ref[...], normed, (((1,), (1,)), ((), ())), preferred_element_type=jnp.float32
        )
        gate = 0.5 * jnp.tanh(0.5 * both[hidden:]) + 0.5
        slab[x] = gate * (both[:hidden] * mask_ref[pl.ds(base + x, 1), :])
        return carry

    lax.fori_loop(0, STEP, row, None, unroll=4)
    for c in range(0, hidden, 16):
        left[c : c + 16, pl.ds(base, STEP), :] = jnp.swapaxes(slab[:, c : c + 16, :], 0, 1).astype(
            jnp.bfloat16
        )

    @pl.when(at == parts * steps - 1)
    def _():
        def head(h, carry):
            out_ref[h] = lax.dot_general(
                right_ref[h], left[h], (((1,), (1,)), ((), ())), preferred_element_type=jnp.float32
            )
            return carry

        lax.fori_loop(0, hidden, head, None, unroll=4)


def left_product(blocks, place, mask, gain, weight, right):
    parts = len(blocks)
    rows, depth, channels = blocks[0].shape
    steps = rows // STEP
    hidden, wide, _ = right.shape
    width = parts * rows

    def part_spec(part):
        return pl.BlockSpec(
            (STEP, depth, channels), lambda g, p: (jnp.clip(g - part * steps, 0, steps - 1), 0, 0)
        )

    def whole(a):
        return pl.BlockSpec(a.shape, lambda g, p: (0,) * a.ndim)

    return pl.pallas_call(
        functools.partial(left_kernel, parts, steps),
        grid_spec=pltpu.PrefetchScalarGridSpec(
            num_scalar_prefetch=1,
            grid=(parts * steps,),
            in_specs=[part_spec(i) for i in range(parts)]
            + [whole(mask), whole(gain), whole(weight), whole(right)],
            out_specs=pl.BlockSpec((hidden, wide, width), lambda g, p: (0, 0, 0)),
            scratch_shapes=[
                pltpu.VMEM((STEP, depth, channels), jnp.bfloat16),
                pltpu.VMEM((STEP, hidden, depth), jnp.float32),
                pltpu.VMEM((hidden, width, depth), jnp.bfloat16),
            ],
        ),
        out_shape=jax.ShapeDtypeStruct((hidden, wide, width), jnp.float32),
        compiler_params=pltpu.CompilerParams(
            vmem_limit_bytes=50 * 2**20, dimension_semantics=("arbitrary",)
        ),
        cost_estimate=pl.CostEstimate(
            flops=32 * width * depth * (channels * 2 * hidden + hidden * wide),
            bytes_accessed=20 * 2**20,
            transcendentals=width * depth * hidden,
        ),
    )(place, *blocks, mask, gain, weight, right)


def norm_last(values, gains):
    average = jnp.mean(values, axis=-1, keepdims=True)
    centred = values - average
    spread = jnp.mean(centred * centred, axis=-1, keepdims=True)
    return centred * lax.rsqrt(spread + 1e-05) * gains


def norm_first(values, gains):
    average = jnp.mean(values, axis=0, keepdims=True)
    centred = values - average
    spread = jnp.mean(centred * centred, axis=0, keepdims=True)
    return centred * lax.rsqrt(spread + 1e-05) * gains[:, None, None]


def body(
    pair,
    token_mask,
    in_gain,
    left_proj,
    left_gate,
    right_proj,
    right_gate,
    out_gate,
    out_gain,
    out_proj,
):
    n_rows = lax.axis_size("rows")
    n_cols = lax.axis_size("cols")
    assert n_rows % 4 == 0 and n_cols == 2
    n_pairs = n_rows // 2
    half_pairs = n_pairs // 2
    rows_tile, cols_tile, channels = pair.shape
    row_at = lax.axis_index("rows")
    col_at = lax.axis_index("cols")
    pair_at, side_at = row_at // 2, row_at % 2

    mask_values = token_mask.astype(jnp.float32)
    mask_cols = lax.dynamic_slice_in_dim(mask_values, col_at * cols_tile, cols_tile)

    def along(block, step):
        return lax.ppermute(
            block, "rows", [(r, (r + 2 * step) % n_rows) for r in range(n_rows)]
        )

    def across(block):
        return lax.ppermute(block, "rows", [(r, r ^ 1) for r in range(n_rows)])

    def sibling(block):
        return lax.ppermute(block, "cols", [(0, 1), (1, 0)])

    chunk_rows = rows_tile // CHUNKS
    own = [pair[n * chunk_rows : (n + 1) * chunk_rows] for n in range(CHUNKS)]
    mine, other = {}, {}
    for d in range(n_pairs):
        for n in range(CHUNKS):
            mine[d, n] = own[n] if d == 0 else along(mine[d - 1, n], 1)
            other[d, n] = across(mine[d, n])

    def gated(normed, w_proj, w_gate, pair_mask):
        projected = jnp.einsum("xkd,dh->hxk", normed, w_proj, preferred_element_type=jnp.float32)
        gate_logits = jnp.einsum("xkd,dh->hxk", normed, w_gate, preferred_element_type=jnp.float32)
        return (jax.nn.sigmoid(gate_logits) * projected * pair_mask[None]).astype(jnp.bfloat16)

    def normalise(values):
        return norm_last(values.astype(jnp.float32), in_gain).astype(jnp.bfloat16)

    mask_rows = lax.dynamic_slice_in_dim(mask_values, row_at * rows_tile, rows_tile)
    right_side = gated(
        normalise(pair), right_proj, right_gate, mask_rows[:, None] * mask_cols[None, :]
    )
    width = 2 * rows_tile

    left_weight = jnp.concatenate([left_proj, left_gate], axis=1).T
    place = (side_at * rows_tile).astype(jnp.int32)[None]

    def source_pair(d):
        return lax.rem(pair_at - d + n_pairs, n_pairs)

    def halves(d):
        mine_at = source_pair(d) * width + side_at * rows_tile
        other_at = source_pair(d) * width + (1 - side_at) * rows_tile
        return (mine, mine_at), (other, other_at)

    def product_of(d, held, first_row, spot):
        rows_mask = lax.dynamic_slice_in_dim(mask_values, first_row, rows_tile)
        return left_product(
            [held[d, n] for n in range(CHUNKS)],
            spot,
            rows_mask[:, None] * mask_cols[None, :],
            in_gain[None],
            left_weight,
            right_side,
        )

    def product(d):
        rows_mask = lax.dynamic_slice_in_dim(mask_values, source_pair(d) * width, width)
        blocks = [mine[d, n] for n in range(CHUNKS)] + [other[d, n] for n in range(CHUNKS)]
        spot = place
        if d == n_pairs - 2:
            arrived = [mine[d + 1, n] for n in range(CHUNKS)]
            spot = lax.optimization_barrier((place, *arrived))[0]
        return left_product(
            blocks,
            spot,
            rows_mask[:, None] * mask_cols[None, :],
            in_gain[None],
            left_weight,
            right_side,
        )

    def last_product(d, earlier):
        start = jnp.zeros((1,), jnp.int32)
        later = lax.optimization_barrier((start, earlier))[0]
        (held, held_at), (swapped, swapped_at) = halves(d)
        held_sum = product_of(d, held, held_at, start)
        swapped_sum = product_of(d, swapped, swapped_at, later)
        first = jnp.where(side_at == 0, held_sum, swapped_sum)
        second = jnp.where(side_at == 0, swapped_sum, held_sum)
        return jnp.concatenate([first, second], axis=2)

    column_at = lax.rem(row_at * rows_tile, cols_tile)
    column_core = (row_at * rows_tile) // cols_tile

    def columns_of(d):
        def cut(chunks):
            return jnp.concatenate(
                [lax.dynamic_slice_in_dim(c, column_at, rows_tile, 1) for c in chunks], axis=0
            )

        held = cut([mine[d, n] for n in range(CHUNKS)])
        swapped = cut([other[d, n] for n in range(CHUNKS)])
        first = jnp.where(side_at == 0, held, swapped)
        second = jnp.where(side_at == 0, swapped, held)
        return jnp.concatenate([first, second], axis=0)

    products = [product(d) for d in range(n_pairs - 1)]
    out = jnp.zeros((rows_tile, cols_tile, channels), jnp.bfloat16)
    for d in range(half_pairs):
        keep_near = source_pair(d) // half_pairs == col_at
        near_pair, far_pair = columns_of(d), columns_of(d + half_pairs)
        kept_pair = jnp.where(keep_near, near_pair, far_pair)
        got_pair = sibling(jnp.where(keep_near, far_pair, near_pair))
        turned = jnp.where(column_core == col_at, kept_pair, got_pair)
        gate_values = jax.nn.sigmoid(
            jnp.einsum(
                "ijd,dc->jic", normalise(turned), out_gate, preferred_element_type=jnp.float32
            )
        )
        if d == half_pairs - 1:
            products.append(last_product(n_pairs - 1, out))
        near_sum, far_sum = products[d], products[d + half_pairs]
        got_sum = sibling(jnp.where(keep_near, far_sum, near_sum).astype(jnp.bfloat16))
        combined = jnp.where(keep_near, near_sum, far_sum) + got_sum.astype(jnp.float32)
        combined_norm = norm_first(combined, out_gain).astype(jnp.bfloat16)
        update = jnp.einsum(
            "hji,hd->jid", combined_norm, out_proj, preferred_element_type=jnp.float32
        )
        swapped = jnp.transpose(turned, (1, 0, 2)).astype(jnp.float32)
        result = (swapped + gate_values * update).astype(jnp.bfloat16)
        spot = lax.rem(pair_at - d + n_pairs, half_pairs)
        out = lax.dynamic_update_slice(out, result, (0, spot * width, 0))
    return out


def solution(mesh):
    return jax.shard_map(
        body,
        mesh=mesh,
        in_specs=(
            P(("crops", "rows"), "cols", None),
            P("crops"),
            P(),
            P(),
            P(),
            P(),
            P(),
            P(),
            P(),
            P(),
        ),
        out_specs=P(("crops", "rows"), "cols", None),
        check_vma=False,
    )
```
